32 devices in a mesh: grp: 2 (over y), box: 4 (over z), lvl: 2 (over x), rhs: 2 (over core).
Axes of the slice: x: 2, y: 2, z: 4, core: 2. Of those that a mesh axis runs over, the one named last changes fastest.
Arguments:
- charges: bfloat16 [64, 16384], P('rhs', ('grp', 'box', 'lvl')), parts along dimension 1, may hold values from -6 to 6
- counts: int32 [256], P(('grp', 'box', 'lvl')), parts along dimension 0, may hold values from 8 to 64
- basis: bfloat16 [256, 64, 64], P(('grp', 'box', 'lvl')), parts along dimension 0, may hold values from -0.75 to 0.75
- transfer: bfloat16 [256, 64, 64], P(('grp', 'box', 'lvl')), parts along dimension 0, may hold values from -0.25 to 0.25
- far_coupling: bfloat16 [256, 20, 64, 64], P(('grp', 'box', 'lvl')), parts along dimension 0, may hold values from -0.15625 to 0.15625
- far_list: int32 [256, 12], P(('grp', 'box', 'lvl')), parts along dimension 0, may hold values from 0 to 127, as said below
- far_slot: int32 [256, 8], P(('grp', 'box', 'lvl')), parts along dimension 0, may hold values from 0 to 7, as said below
- send_rows: int32 [16, 8, 1], P(('grp', 'box', 'lvl')), parts along dimension 0, may hold values from 0 to 15
- coarse_coupling: bfloat16 [32, 4, 64, 64], P(('grp', 'box', 'lvl')), parts along dimension 0, may hold values from -0.375 to 0.375
- near_blocks: bfloat16 [256, 9, 64, 64], P(('grp', 'box', 'lvl')), parts along dimension 0, may hold values from -0.25 to 0.25
- near_list: int32 [256, 9], P(('grp', 'box', 'lvl')), parts along dimension 0, may hold values from 0 to 127, as said below
Outputs:
- potential: bfloat16 [64, 16384], P('rhs', ('grp', 'box', 'lvl')), parts along dimension 1
The draws below stay inside these ranges and needn't reach their ends.
There are 2 independent parts, one for each index of `grp`. The reference program is written for one: setup_inputs(seed, part) draws one part's arguments, and reference() takes and returns one part's arrays. A program takes and returns all parts, laid end to end along the dimension named above; each array names one. Nothing has to cross between parts.
Inputs may be any that keep to these rules, and one draw needn't show every extreme that they name: `near_list`: entries lie within 4 leaf boxes of the row's own leaf box; the first entry of each row is the leaf box itself. `far_list`: entries of row l name leaf boxes held by index l // 16 of box and lvl or by the index just before or after it. `far_slot`: each index's rows name every slot of the 8 it receives.
All inputs are finite; a program needn't handle non-finite values.
Results may differ from the reference program's by a relative error of at most 0.0053.
Values may be sent and summed in bfloat16 or wider, within the bound.
A program may use at most 128 MiB of HBM per device.

```python
import jax
import jax.numpy as jnp
from jax import lax

PTS = 64
RANK = 64
NRHS = 64
LEAF_DEV = 16
FAR_WIN = 12
FAR_TAIL = 8
NEAR = 9
HALO = 4
CAP = 1
FAR = 20
DEVS = 8
NLEAF = 128
NPTS = 8192
NPAR = 16
GPAR = 4


def draw_far_slot(key, part):
    key = jax.random.fold_in(key, 7)
    keys = jax.random.split(key, DEVS)
    orders = jax.vmap(lambda single: jax.random.permutation(single, LEAF_DEV * FAR_TAIL))(keys)
    slots = orders % (DEVS * CAP)
    return slots.reshape(NLEAF, FAR_TAIL).astype(jnp.int32)


def draw_far_list(key, part):
    key = jax.random.fold_in(key, 13)
    first_key, second_key = jax.random.split(key)
    leaves = jnp.arange(NLEAF)[:, None]
    device = leaves // LEAF_DEV
    column = jnp.arange(FAR_WIN)[None, :]
    choose = jax.random.randint(first_key, (NLEAF, FAR_WIN), 0, 4)
    moved = jnp.where(choose == 2, -1, jnp.where(choose == 3, 1, 0))
    moved = jnp.where(column == 0, -1, jnp.where(column == 1, 1, moved))
    target = device + moved
    target = jnp.where((target < 0) | (target >= DEVS), device - moved, target)
    within = jax.random.randint(second_key, (NLEAF, FAR_WIN), 0, LEAF_DEV)
    within = jnp.where(column < 2, leaves % LEAF_DEV, within)
    return (target * LEAF_DEV + within).astype(jnp.int32)


def draw_near_list(key, part):
    key = jax.random.fold_in(key, 11)
    leaves = jnp.arange(NLEAF)[:, None]
    offsets = jax.random.randint(key, (NLEAF, NEAR), -HALO, HALO + 1)
    column = jnp.arange(NEAR)[None, :]
    offsets = jnp.where(column == 0, 0, jnp.where(column == 1, -HALO, jnp.where(column == 2, HALO, offsets)))
    target = leaves + offsets
    target = jnp.where((target < 0) | (target >= NLEAF), leaves - offsets, target)
    return target.astype(jnp.int32)


def touch_ends(result, key, least, top_value):
    shape = result.shape
    place = [jax.random.randint(jax.random.fold_in(key, axis), (), 0, shape[axis]) for axis in range(len(shape))]
    result = result.at[tuple(place)].set(least)
    longest = shape.index(max(shape))
    place[longest] = (place[longest] + 1) % shape[longest]
    return result.at[tuple(place)].set(top_value)


def steps_of(stream_key, shape, cuts, least, largest):
    level = 1.0
    for axis_at, shards_of in cuts:
        draws = jax.random.uniform(jax.random.fold_in(jax.random.fold_in(stream_key, 6), axis_at), (shards_of,), jnp.float32, least / len(cuts), largest / len(cuts))
        level = level * jnp.repeat(jnp.exp(draws), shape[axis_at] // shards_of).reshape((-1,) + (1,) * (len(shape) - 1 - axis_at))
    return level


def centred(stream_key, shape, deviation, reach, shards=(), kind=jnp.bfloat16):
    drawn = deviation * jax.random.normal(stream_key, shape, jnp.float32)
    if shards:
        drawn = drawn * steps_of(stream_key, shape, shards, -0.22, 0.18)
    return jnp.clip(drawn, -reach, reach).astype(kind)


def setup_inputs(seed: int = 0, part: int = 0) -> dict:
    splits = jax.random.split(jax.random.key(seed), 12)
    part_splits = jax.random.split(jax.random.fold_in(splits[11], part), 12)
    return {
        "charges": centred(part_splits[0], (NRHS, NPTS), 1.0, 6.0, ((0, 2), (1, 8))),
        "counts": touch_ends(jax.random.randint(part_splits[1], (NLEAF,), 8, PTS + 1), jax.random.fold_in(part_splits[1], 1), 8, PTS).astype(jnp.int32),
        "basis": centred(part_splits[2], (NLEAF, PTS, RANK), PTS ** -0.5, 0.75, ((0, 8),)),
        "transfer": centred(part_splits[3], (NLEAF, RANK, RANK), (8 * RANK) ** -0.5, 0.25, ((0, 8),)),
        "far_coupling": centred(part_splits[4], (NLEAF, FAR, RANK, RANK), (FAR * RANK) ** -0.5, 0.15625, ((0, 8),)),
        "far_list": draw_far_list(jax.random.fold_in(jax.random.fold_in(splits[11], part), 71), part),
        "far_slot": draw_far_slot(jax.random.fold_in(jax.random.fold_in(splits[11], part), 71), part),
        "send_rows": touch_ends(jax.random.randint(part_splits[7], (DEVS, DEVS, CAP), 0, LEAF_DEV), jax.random.fold_in(part_splits[7], 1), 0, LEAF_DEV - 1).astype(jnp.int32),
        "coarse_coupling": centred(part_splits[8], (NPAR, GPAR, RANK, RANK), (GPAR * RANK) ** -0.5, 0.375, ((0, 8),)),
        "near_blocks": centred(part_splits[9], (NLEAF, NEAR, PTS, PTS), (NEAR * PTS) ** -0.5, 0.25, ((0, 8),)),
        "near_list": draw_near_list(jax.random.fold_in(jax.random.fold_in(splits[11], part), 71), part),
    }


def reference(charges, counts, basis, transfer, far_coupling, far_list, far_slot, send_rows, coarse_coupling, near_blocks, near_list):
    live = jnp.arange(PTS)[None, :] < counts[:, None]
    blocks = charges.reshape(NRHS, NLEAF, PTS)
    masked = jnp.where(live[None], blocks, jnp.zeros((), charges.dtype))
    coef = jnp.einsum('lpr,clp->lcr', basis.astype(jnp.float32), masked.astype(jnp.float32)).astype(jnp.bfloat16)
    tr_groups = transfer.reshape(NPAR, 8, RANK, RANK).astype(jnp.float32)
    upward = jnp.einsum('nkrs,nkcr->ncs', tr_groups, coef.reshape(NPAR, 8, NRHS, RANK).astype(jnp.float32)).astype(jnp.bfloat16)
    coef_wide = coef.astype(jnp.float32)

    def far_block(items):
        coupling_block, list_block, slot_block, device = items
        window = jnp.einsum('lkrs,lkcs->lcr', coupling_block[:, :FAR_WIN].astype(jnp.float32), coef_wide[list_block])
        peer = slot_block // CAP
        within = slot_block % CAP
        source = peer * LEAF_DEV + send_rows[peer, device, within]
        picked = coef_wide[source]
        tail = jnp.einsum('lkrs,lkcs->lcr', coupling_block[:, FAR_WIN:].astype(jnp.float32), picked)
        return window + tail

    farfield = lax.map(far_block, (far_coupling.reshape(DEVS, LEAF_DEV, FAR, RANK, RANK), far_list.reshape(DEVS, LEAF_DEV, FAR_WIN), far_slot.reshape(DEVS, LEAF_DEV, FAR_TAIL), jnp.arange(DEVS).astype(jnp.int32)))
    farfield = farfield.reshape(NLEAF, NRHS, RANK)
    groups = upward.reshape(NPAR // GPAR, GPAR, NRHS, RANK).astype(jnp.float32)
    coupling_groups = coarse_coupling.reshape(NPAR // GPAR, GPAR, GPAR, RANK, RANK).astype(jnp.float32)
    coarse = jnp.einsum('gtsrq,gscq->gtcr', coupling_groups, groups).reshape(NPAR, NRHS, RANK).astype(jnp.bfloat16)
    downward = jnp.einsum('nkrs,ncs->nkcr', tr_groups, coarse.astype(jnp.float32)).reshape(NLEAF, NRHS, RANK)
    local = (farfield + downward).astype(jnp.bfloat16)
    far_part = jnp.einsum('lpr,lcr->clp', basis.astype(jnp.float32), local.astype(jnp.float32))
    masked_wide = masked.astype(jnp.float32)

    def near_block(items):
        near_group, list_group = items
        picked = masked_wide[:, list_group]
        return jnp.einsum('ljpq,cljq->clp', near_group.astype(jnp.float32), picked)

    near_part = lax.map(near_block, (near_blocks.reshape(DEVS, LEAF_DEV, NEAR, PTS, PTS), near_list.reshape(DEVS, LEAF_DEV, NEAR)))
    near_part = jnp.transpose(near_part, (1, 0, 2, 3)).reshape(NRHS, NLEAF, PTS)
    total = jnp.where(live[None], near_part + far_part, jnp.zeros((), jnp.float32))
    return total.reshape(NRHS, NPTS).astype(jnp.bfloat16)
```

```python
import functools

import jax
import jax.numpy as jnp
from jax import lax
from jax.experimental import pallas as pl
from jax.experimental.pallas import tpu as pltpu
from jax.sharding import PartitionSpec as P

HALO = 4
FAMILY = 8
MESH = pl.DeviceIdType.MESH
UNROLL = 1


def nn(a, b):
    return lax.dot_general(a, b, (((1,), (0,)), ((), ())), preferred_element_type=jnp.float32)


def nt(a, b):
    return lax.dot_general(a, b, (((1,), (1,)), ((), ())), preferred_element_type=jnp.float32)


def kernel(
    lvl_count,
    index_count,
    charges_hbm,
    counts_hbm,
    basis_hbm,
    transfer_hbm,
    far_hbm,
    far_list_hbm,
    far_slot_hbm,
    rows_hbm,
    coarse_hbm,
    near_hbm,
    near_list_hbm,
    out_ref,
    charges,
    basis,
    transfer,
    far,
    coupling,
    near,
    counts,
    far_list,
    far_slot,
    rows,
    near_list,
    cells,
    own,
    window,
    stage,
    tail,
    up_own,
    up_all,
    coarse,
    near_sum,
    load_sem,
    halo_send,
    halo_recv,
    win_send,
    win_recv,
    tail_send,
    tail_recv,
    up_send,
    up_recv,
):
    box = lax.axis_index("box")
    lvl = lax.axis_index("lvl")
    me = box * lvl_count + lvl
    leaf_dev, points, rank = basis.shape
    win_count = far_list.shape[1]
    tail_count = far_slot.shape[0]
    near_count = near.shape[1]
    cap = rows.shape[1]
    parents = up_own.shape[0]
    group = coupling.shape[1]
    wide = 2 * points
    cell_ring = cells.shape[0]
    win_ring = window.shape[0]
    cell_home = lax.rem(me, 2) * leaf_dev
    win_home = lax.rem(me, win_ring // leaf_dev) * leaf_dev

    loads = [
        pltpu.make_async_copy(source, target, load_sem.at[i])
        for i, (source, target) in enumerate(
            (
                (charges_hbm, charges),
                (counts_hbm, counts),
                (basis_hbm, basis),
                (rows_hbm, rows),
                (transfer_hbm, transfer),
                (near_list_hbm, near_list),
                (near_hbm, near),
                (coarse_hbm, coupling),
                (far_list_hbm, far_list),
                (far_slot_hbm, far_slot),
                (far_hbm, far),
            )
        )
    ]
    for load in loads:
        load.start()

    def place(index):
        return {"box": lax.div(index, lvl_count), "lvl": lax.rem(index, lvl_count)}

    def other(step):
        return lax.rem(me + step, index_count)

    barrier = pltpu.get_barrier_semaphore()

    @pl.loop(1, index_count)
    def _(step):
        pl.semaphore_signal(barrier, inc=1, device_id=place(other(step)), device_id_type=MESH)

    has_prev = me > 0
    has_next = me < index_count - 1
    prev_place = place(lax.max(me - 1, 0))
    next_place = place(lax.min(me + 1, index_count - 1))

    def remote(source, target, send, recv, where):
        return pltpu.make_async_remote_copy(
            src_ref=source,
            dst_ref=target,
            send_sem=send,
            recv_sem=recv,
            device_id=where,
            device_id_type=MESH,
        )

    halo_next = remote(
        cells.at[pl.ds(cell_home + leaf_dev - HALO, HALO)],
        cells.at[pl.ds(cell_home + leaf_dev - HALO, HALO)],
        halo_send.at[0],
        halo_recv.at[0],
        next_place,
    )
    halo_prev = remote(
        cells.at[pl.ds(cell_home, HALO)],
        cells.at[pl.ds(cell_home, HALO)],
        halo_send.at[1],
        halo_recv.at[1],
        prev_place,
    )
    win_next = remote(own, window.at[pl.ds(win_home, leaf_dev)], win_send.at[0], win_recv.at[0], next_place)
    win_prev = remote(own, window.at[pl.ds(win_home, leaf_dev)], win_send.at[1], win_recv.at[1], prev_place)

    def tail_copy(step):
        peer = other(step)
        return remote(
            stage.at[pl.ds(peer * cap, cap)],
            tail.at[pl.ds(me * cap, cap)],
            tail_send.at[step],
            tail_recv.at[step],
            place(peer),
        )

    def up_copy(step):
        return remote(
            up_own,
            up_all.at[pl.ds(lvl * parents, parents)],
            up_send.at[step],
            up_recv.at[step],
            {"lvl": lax.rem(lvl + step, lvl_count)},
        )

    lanes = lax.broadcasted_iota(jnp.int32, (charges.shape[0], wide), 1)

    def live(pair):
        first = counts[2 * pair]
        second = counts[2 * pair + 1] + points
        return (lanes < first) | ((lanes >= points) & (lanes < second))

    loads[0].wait()
    loads[1].wait()

    for pair in range(leaf_dev // 2):
        block = charges[:, pair * wide : (pair + 1) * wide]
        block = jnp.where(live(pair), block.astype(jnp.float32), 0.0).astype(jnp.bfloat16)
        cells[cell_home + 2 * pair] = block[:, :points]
        cells[cell_home + 2 * pair + 1] = block[:, points:]

    pl.semaphore_wait(barrier, index_count - 1)

    @pl.when(has_next)
    def _():
        halo_next.start()

    @pl.when(has_prev)
    def _():
        halo_prev.start()

    loads[2].wait()

    for leaf in range(leaf_dev):
        value = nn(cells[cell_home + leaf], basis[leaf]).astype(jnp.bfloat16)
        own[leaf] = value
        window[win_home + leaf] = value

    @pl.when(has_next)
    def _():
        win_next.start()

    @pl.when(has_prev)
    def _():
        win_prev.start()

    loads[3].wait()

    @pl.loop(1, index_count)
    def _(step):
        peer = other(step)
        for j in range(cap):
            stage[peer * cap + j] = own[rows[0, j, peer]]
        tail_copy(step).start()

    for j in range(cap):
        tail[me * cap + j] = own[rows[0, j, me]]

    loads[4].wait()
    for parent in range(parents):
        total = None
        for k in range(FAMILY):
            leaf = parent * FAMILY + k
            term = nn(own[leaf], transfer[leaf])
            total = term if total is None else total + term
        value = total.astype(jnp.bfloat16)
        up_own[parent] = value
        up_all[lvl * parents + parent] = value

    @pl.loop(1, lvl_count)
    def _(step):
        up_copy(step).start()

    loads[5].wait()
    loads[6].wait()

    @pl.when(has_prev)
    def _():
        halo_next.wait_recv()

    @pl.when(has_next)
    def _():
        halo_prev.wait_recv()

    def near_body(pair, _):
        sums = []
        for half in range(2):
            leaf = 2 * pair + half
            total = None
            for k in range(near_count):
                source = near_list[leaf, k] & (cell_ring - 1)
                term = nt(cells[source], near[leaf, k])
                total = term if total is None else total + term
            sums.append(total)
        near_sum[pair] = jnp.concatenate(sums, axis=1)
        return _

    lax.fori_loop(0, leaf_dev // 2, near_body, 0, unroll=UNROLL)

    loads[7].wait()

    @pl.loop(1, lvl_count)
    def _(step):
        up_copy(step).wait_recv()

    for parent in range(parents):
        total = None
        for k in range(group):
            term = nt(up_all[k], coupling[parent, k])
            total = term if total is None else total + term
        coarse[parent] = total.astype(jnp.bfloat16)

    loads[8].wait()
    loads[9].wait()
    loads[10].wait()

    @pl.when(has_prev)
    def _():
        win_next.wait_recv()

    @pl.when(has_next)
    def _():
        win_prev.wait_recv()

    @pl.loop(1, index_count)
    def _(step):
        tail_copy(step).wait_recv()

    def far_body(pair, _):
        parts = []
        for half in range(2):
            leaf = 2 * pair + half
            total = nt(coarse[lax.div(pair, FAMILY // 2)], transfer[leaf])
            for k in range(win_count):
                source = far_list[leaf, k] & (win_ring - 1)
                total = total + nt(window[source], far[leaf, k])
            for k in range(tail_count):
                total = total + nt(tail[far_slot[k, leaf]], far[leaf, win_count + k])
            parts.append(nt(total.astype(jnp.bfloat16), basis[leaf]))
        total = near_sum[pair] + jnp.concatenate(parts, axis=1)
        total = jnp.where(live(pair), total, 0.0)
        out_ref[:, pl.ds(pl.multiple_of(pair * wide, wide), wide)] = total.astype(jnp.bfloat16)
        return _

    lax.fori_loop(0, leaf_dev // 2, far_body, 0, unroll=UNROLL)

    @pl.when(has_next)
    def _():
        halo_next.wait_send()
        win_next.wait_send()

    @pl.when(has_prev)
    def _():
        halo_prev.wait_send()
        win_prev.wait_send()

    @pl.loop(1, index_count)
    def _(step):
        tail_copy(step).wait_send()

    @pl.loop(1, lvl_count)
    def _(step):
        up_copy(step).wait_send()


def on_device(
    lvl_count,
    index_count,
    charges,
    counts,
    basis,
    transfer,
    far_coupling,
    far_list,
    far_slot,
    send_rows,
    coarse_coupling,
    near_blocks,
    near_list,
):
    columns = charges.shape[0]
    leaf_dev, points, rank = basis.shape
    parents, group = coarse_coupling.shape[:2]
    cap = send_rows.shape[2]
    far_slot = far_slot.T
    send_rows = send_rows.transpose(0, 2, 1)
    half = jnp.bfloat16

    def cell(count):
        return pltpu.VMEM((count, columns, rank), half)

    dma = pltpu.SemaphoreType.DMA
    return pl.pallas_call(
        functools.partial(kernel, lvl_count, index_count),
        out_shape=jax.ShapeDtypeStruct(charges.shape, half),
        in_specs=[pl.BlockSpec(memory_space=pl.ANY)] * 11,
        out_specs=pl.BlockSpec(memory_space=pltpu.VMEM),
        scratch_shapes=[
            pltpu.VMEM(charges.shape, half),
            pltpu.VMEM(basis.shape, half),
            pltpu.VMEM(transfer.shape, half),
            pltpu.VMEM(far_coupling.shape, half),
            pltpu.VMEM(coarse_coupling.shape, half),
            pltpu.VMEM(near_blocks.shape, half),
            pltpu.SMEM(counts.shape, jnp.int32),
            pltpu.SMEM(far_list.shape, jnp.int32),
            pltpu.SMEM(far_slot.shape, jnp.int32),
            pltpu.SMEM(send_rows.shape, jnp.int32),
            pltpu.SMEM(near_list.shape, jnp.int32),
            cell(2 * leaf_dev),
            cell(leaf_dev),
            cell(4 * leaf_dev),
            cell(index_count * cap),
            cell(index_count * cap),
            cell(parents),
            cell(group),
            cell(parents),
            pltpu.VMEM((leaf_dev // 2, columns, 2 * points), jnp.float32),
            dma((11,)),
            dma((2,)),
            dma((2,)),
            dma((2,)),
            dma((2,)),
            dma((index_count,)),
            dma((index_count,)),
            dma((lvl_count,)),
            dma((lvl_count,)),
        ],
        compiler_params=pltpu.CompilerParams(
            collective_id=0, has_side_effects=True, vmem_limit_bytes=48 * 1024 * 1024
        ),
    )(
        charges,
        counts,
        basis,
        transfer,
        far_coupling,
        far_list,
        far_slot,
        send_rows,
        coarse_coupling,
        near_blocks,
        near_list,
    )


def solution(mesh):
    every = ("grp", "box", "lvl")
    placed = (
        P("rhs", every),
        P(every),
        P(every, None, None),
        P(every, None, None),
        P(every, None, None, None),
        P(every, None),
        P(every, None),
        P(every, None, None),
        P(every, None, None, None),
        P(every, None, None, None),
        P(every, None),
    )
    lvl_count = mesh.shape["lvl"]
    return jax.shard_map(
        functools.partial(on_device, lvl_count, lvl_count * mesh.shape["box"]),
        mesh=mesh,
        in_specs=placed,
        out_specs=P("rhs", every),
        check_vma=False,
    )
```

```python
import functools

import jax
import jax.numpy as jnp
from jax import lax
from jax.experimental import pallas as pl
from jax.experimental.pallas import tpu as pltpu
from jax.sharding import PartitionSpec as P

HALO = 4
FAMILY = 8
MESH = pl.DeviceIdType.MESH


def nn(a, b):
    return lax.dot_general(a, b, (((1,), (0,)), ((), ())), preferred_element_type=jnp.float32)


def packed(blocks):
    return jnp.concatenate(blocks, axis=1)


def stacked(blocks):
    return jnp.concatenate(blocks, axis=0)


def kernel(
    lvl_count,
    index_count,
    charges_hbm,
    counts_hbm,
    basis_hbm,
    transfer_hbm,
    far_hbm,
    far_list_hbm,
    far_slot_hbm,
    rows_hbm,
    coarse_hbm,
    near_hbm,
    near_list_hbm,
    out_ref,
    charges,
    basis,
    transfer,
    far,
    coupling,
    near,
    counts,
    far_list,
    far_slot,
    rows,
    near_list,
    masked,
    halo,
    own,
    own_flat,
    stage,
    arrived,
    tail_in,
    up_own,
    up_in,
    cells,
    window,
    tail,
    up_all,
    coarse,
    far_packed,
    near_packed,
    near_sum,
    load_sem,
    halo_send,
    halo_recv,
    win_send,
    win_recv,
    tail_send,
    tail_recv,
    up_send,
    up_recv,
):
    box = lax.axis_index("box")
    lvl = lax.axis_index("lvl")
    me = box * lvl_count + lvl
    leaf_dev, points, rank = basis.shape
    columns = charges.shape[0]
    pairs = leaf_dev // 2
    edge = HALO // 2
    far_count = far.shape[1]
    win_count = far_list.shape[1]
    near_count = near.shape[1]
    near_even = near_count // 2 * 2
    cap = rows.shape[1]
    parents = coarse.shape[0]
    group = coupling.shape[1]
    wide = 2 * points
    cell_ring = cells.shape[0]
    win_ring = window.shape[0]
    cell_home = lax.rem(me, 2) * leaf_dev
    cell_away = leaf_dev - cell_home
    blocks = win_ring // leaf_dev
    win_home = lax.rem(me, blocks) * leaf_dev
    win_prev_home = lax.rem(me + blocks - 1, blocks) * leaf_dev
    win_next_home = lax.rem(me + 1, blocks) * leaf_dev

    loads = {}
    for i, (source, target) in enumerate(
        (
            (charges_hbm, charges),
            (counts_hbm, counts),
            (basis_hbm, basis),
            (rows_hbm, rows),
            (transfer_hbm, transfer),
            (near_list_hbm, near_list),
            (near_hbm, near),
            (coarse_hbm, coupling),
            (far_list_hbm, far_list),
            (far_slot_hbm, far_slot),
            (far_hbm, far),
        )
    ):
        loads[i] = pltpu.make_async_copy(source, target, load_sem.at[i])
        loads[i].start()

    def place(index):
        return {"box": lax.div(index, lvl_count), "lvl": lax.rem(index, lvl_count)}

    def other(step):
        return lax.rem(me + step, index_count)

    barrier = pltpu.get_barrier_semaphore()

    @pl.loop(1, index_count)
    def _(step):
        pl.semaphore_signal(barrier, inc=1, device_id=place(other(step)), device_id_type=MESH)

    has_prev = me > 0
    has_next = me < index_count - 1
    prev_place = place(lax.max(me - 1, 0))
    next_place = place(lax.min(me + 1, index_count - 1))

    def remote(source, target, send, recv, where):
        return pltpu.make_async_remote_copy(
            src_ref=source,
            dst_ref=target,
            send_sem=send,
            recv_sem=recv,
            device_id=where,
            device_id_type=MESH,
        )

    halo_next = remote(
        masked.at[pl.ds(pairs - edge, edge)], halo.at[0], halo_send.at[0], halo_recv.at[0], next_place
    )
    halo_prev = remote(masked.at[pl.ds(0, edge)], halo.at[1], halo_send.at[1], halo_recv.at[1], prev_place)
    win_next = remote(own, arrived.at[0], win_send.at[0], win_recv.at[0], next_place)
    win_prev = remote(own, arrived.at[1], win_send.at[1], win_recv.at[1], prev_place)

    def tail_copy(step):
        peer = other(step)
        return remote(
            stage.at[pl.ds(peer * cap, cap)],
            tail_in.at[pl.ds(me * cap, cap)],
            tail_send.at[step],
            tail_recv.at[step],
            place(peer),
        )

    def up_copy(step):
        return remote(
            up_own,
            up_in.at[lvl],
            up_send.at[step],
            up_recv.at[step],
            {"lvl": lax.rem(lvl + step, lvl_count)},
        )

    lanes = lax.broadcasted_iota(jnp.int32, (columns, wide), 1)

    def live(pair):
        first = counts[2 * pair]
        second = counts[2 * pair + 1] + points
        return (lanes < first) | ((lanes >= points) & (lanes < second))

    def spread(pair_block, target, at):
        turned = pair_block.T
        target[at] = turned[:points]
        target[at + 1] = turned[points:]

    loads[0].wait()
    loads[1].wait()

    for pair in range(pairs):
        block = charges[:, pair * wide : (pair + 1) * wide]
        masked[pair] = jnp.where(live(pair), block.astype(jnp.float32), 0.0).astype(jnp.bfloat16)

    loads[2].wait()

    for pair in range(pairs):
        block = masked[pair]
        first = nn(block[:, :points], basis[2 * pair])
        second = nn(block[:, points:], basis[2 * pair + 1])
        own[pair] = packed([first, second]).astype(jnp.bfloat16)
        for half, value in enumerate((first, second)):
            value = value.astype(jnp.bfloat16)
            own_flat[2 * pair + half] = packed([value[: columns // 2], value[columns // 2 :]])

    pl.semaphore_wait(barrier, index_count - 1)

    @pl.when(has_next)
    def _():
        halo_next.start()
        win_next.start()

    @pl.when(has_prev)
    def _():
        halo_prev.start()
        win_prev.start()

    loads[4].wait()
    sums = []
    for parent in range(parents):
        total = None
        for k in range(FAMILY // 2):
            pair = parent * (FAMILY // 2) + k
            block = own[pair]
            term = nn(block[:, :rank], transfer[2 * pair]) + nn(block[:, rank:], transfer[2 * pair + 1])
            total = term if total is None else total + term
        sums.append(total)
    for half in range(parents // 2):
        value = packed(sums[2 * half : 2 * half + 2]).astype(jnp.bfloat16)
        up_own[half] = value
        up_in[lvl, half] = value

    @pl.loop(1, lvl_count)
    def _(step):
        up_copy(step).start()

    loads[3].wait()

    @pl.loop(1, index_count)
    def _(step):
        peer = other(step)
        for j in range(cap):
            stage[peer * cap + j] = own_flat[rows[0, j, peer]]
        tail_copy(step).start()

    for j in range(cap):
        tail_in[me * cap + j] = own_flat[rows[0, j, me]]

    for pair in range(pairs):
        spread(masked[pair], cells, cell_home + 2 * pair)
        spread(own[pair], window, win_home + 2 * pair)

    loads[5].wait()
    loads[6].wait()

    @pl.when(has_prev)
    def _():
        halo_next.wait_recv()
        for pair in range(edge):
            spread(halo[0, pair], cells, cell_away + leaf_dev - HALO + 2 * pair)

    @pl.when(has_next)
    def _():
        halo_prev.wait_recv()
        for pair in range(edge):
            spread(halo[1, pair], cells, cell_away + 2 * pair)

    @pl.loop(0, leaf_dev)
    def _(leaf):
        for k in range(near_even // 2):
            near_packed[leaf, :, k * wide : (k + 1) * wide] = packed([near[leaf, 2 * k], near[leaf, 2 * k + 1]])

    @pl.loop(0, pairs)
    def _(pair):
        for half in range(2):
            leaf = 2 * pair + half
            found = [cells[near_list[leaf, k] & (cell_ring - 1)] for k in range(near_count)]
            total = nn(near_packed[leaf], stacked(found[:near_even]))
            for k in range(near_even, near_count):
                total = total + nn(near[leaf, k], found[k])
            near_sum[leaf] = total

    for i in (7, 8, 9, 10):
        loads[i].wait()

    @pl.loop(0, leaf_dev)
    def _(leaf):
        for k in range(far_count // 2):
            far_packed[leaf, :, k * wide : (k + 1) * wide] = packed([far[leaf, 2 * k], far[leaf, 2 * k + 1]])

    @pl.loop(1, lvl_count)
    def _(step):
        up_copy(step).wait_recv()

    for peer in range(lvl_count):
        for half in range(parents // 2):
            spread(up_in[peer, half], up_all, peer * parents + 2 * half)

    for parent in range(parents):
        total = None
        for k in range(group):
            term = nn(coupling[parent, k], up_all[k])
            total = term if total is None else total + term
        coarse[parent] = total.astype(jnp.bfloat16)

    @pl.loop(1, index_count)
    def _(step):
        tail_copy(step).wait_recv()

    @pl.loop(0, index_count * cap)
    def _(slot):
        turned = tail_in[slot].T
        tail[slot] = packed([turned[:rank], turned[rank:]])

    @pl.when(has_prev)
    def _():
        win_next.wait_recv()
        for pair in range(pairs):
            spread(arrived[0, pair], window, win_prev_home + 2 * pair)

    @pl.when(has_next)
    def _():
        win_prev.wait_recv()
        for pair in range(pairs):
            spread(arrived[1, pair], window, win_next_home + 2 * pair)

    @pl.loop(0, pairs)
    def _(pair):
        parts = []
        for half in range(2):
            leaf = 2 * pair + half
            found = [window[far_list[leaf, k] & (win_ring - 1)] for k in range(win_count)]
            found += [tail[far_slot[k, leaf]] for k in range(far_count - win_count)]
            total = nn(transfer[leaf], coarse[lax.div(pair, FAMILY // 2)])
            total = total + nn(far_packed[leaf], stacked(found))
            parts.append(near_sum[leaf] + nn(basis[leaf], total.astype(jnp.bfloat16)))
        total = jnp.where(live(pair), stacked(parts).T, 0.0)
        out_ref[:, pl.ds(pl.multiple_of(pair * wide, wide), wide)] = total.astype(jnp.bfloat16)

    @pl.when(has_next)
    def _():
        halo_next.wait_send()
        win_next.wait_send()

    @pl.when(has_prev)
    def _():
        halo_prev.wait_send()
        win_prev.wait_send()

    @pl.loop(1, index_count)
    def _(step):
        tail_copy(step).wait_send()

    @pl.loop(1, lvl_count)
    def _(step):
        up_copy(step).wait_send()


def on_device(
    lvl_count,
    index_count,
    charges,
    counts,
    basis,
    transfer,
    far_coupling,
    far_list,
    far_slot,
    send_rows,
    coarse_coupling,
    near_blocks,
    near_list,
):
    columns = charges.shape[0]
    leaf_dev, points, rank = basis.shape
    parents, group = coarse_coupling.shape[:2]
    cap = send_rows.shape[2]
    far_slot = far_slot.T
    send_rows = send_rows.transpose(0, 2, 1)
    half = jnp.bfloat16

    pairs = leaf_dev // 2
    far_wide = far_coupling.shape[1] * rank
    near_wide = near_blocks.shape[1] // 2 * 2 * points

    def turned(count):
        return pltpu.VMEM((count, rank, columns), half)

    dma = pltpu.SemaphoreType.DMA
    return pl.pallas_call(
        functools.partial(kernel, lvl_count, index_count),
        out_shape=jax.ShapeDtypeStruct(charges.shape, half),
        in_specs=[pl.BlockSpec(memory_space=pl.ANY)] * 11,
        out_specs=pl.BlockSpec(memory_space=pltpu.VMEM),
        scratch_shapes=[
            pltpu.VMEM(charges.shape, half),
            pltpu.VMEM(basis.shape, half),
            pltpu.VMEM(transfer.shape, half),
            pltpu.VMEM(far_coupling.shape, half),
            pltpu.VMEM(coarse_coupling.shape, half),
            pltpu.VMEM(near_blocks.shape, half),
            pltpu.SMEM(counts.shape, jnp.int32),
            pltpu.SMEM(far_list.shape, jnp.int32),
            pltpu.SMEM(far_slot.shape, jnp.int32),
            pltpu.SMEM(send_rows.shape, jnp.int32),
            pltpu.SMEM(near_list.shape, jnp.int32),
            pltpu.VMEM((pairs, columns, 2 * points), half),
            pltpu.VMEM((2, HALO // 2, columns, 2 * points), half),
            pltpu.VMEM((pairs, columns, 2 * rank), half),
            pltpu.VMEM((leaf_dev, columns // 2, 2 * rank), half),
            pltpu.VMEM((index_count * cap, columns // 2, 2 * rank), half),
            pltpu.VMEM((2, pairs, columns, 2 * rank), half),
            pltpu.VMEM((index_count * cap, columns // 2, 2 * rank), half),
            pltpu.VMEM((parents // 2, columns, 2 * rank), half),
            pltpu.VMEM((lvl_count, parents // 2, columns, 2 * rank), half),
            turned(2 * leaf_dev),
            turned(4 * leaf_dev),
            turned(index_count * cap),
            turned(group),
            turned(parents),
            pltpu.VMEM((leaf_dev, rank, far_wide), half),
            pltpu.VMEM((leaf_dev, points, near_wide), half),
            pltpu.VMEM((leaf_dev, points, columns), jnp.float32),
            dma((11,)),
            dma((2,)),
            dma((2,)),
            dma((2,)),
            dma((2,)),
            dma((index_count,)),
            dma((index_count,)),
            dma((lvl_count,)),
            dma((lvl_count,)),
        ],
        compiler_params=pltpu.CompilerParams(
            collective_id=0, has_side_effects=True, vmem_limit_bytes=63 * 1024 * 1024
        ),
    )(
        charges,
        counts,
        basis,
        transfer,
        far_coupling,
        far_list,
        far_slot,
        send_rows,
        coarse_coupling,
        near_blocks,
        near_list,
    )


def solution(mesh):
    every = ("grp", "box", "lvl")
    placed = (
        P("rhs", every),
        P(every),
        P(every, None, None),
        P(every, None, None),
        P(every, None, None, None),
        P(every, None),
        P(every, None),
        P(every, None, None),
        P(every, None, None, None),
        P(every, None, None, None),
        P(every, None),
    )
    lvl_count = mesh.shape["lvl"]
    return jax.shard_map(
        functools.partial(on_device, lvl_count, lvl_count * mesh.shape["box"]),
        mesh=mesh,
        in_specs=placed,
        out_specs=P("rhs", every),
        check_vma=False,
    )
```

```python
import functools

import jax
import jax.numpy as jnp
from jax import lax
from jax.experimental import pallas as pl
from jax.experimental.pallas import tpu as pltpu
from jax.sharding import PartitionSpec as P

HALO = 4
FAMILY = 8
MESH = pl.DeviceIdType.MESH


def nn(a, b):
    return lax.dot_general(a, b, (((1,), (0,)), ((), ())), preferred_element_type=jnp.float32)


def packed(blocks):
    return jnp.concatenate(blocks, axis=1)


def stacked(blocks):
    return jnp.concatenate(blocks, axis=0)


def kernel(
    lvl_count,
    index_count,
    charges_hbm,
    counts_hbm,
    basis_hbm,
    transfer_hbm,
    far_hbm,
    far_list_hbm,
    far_slot_hbm,
    rows_hbm,
    coarse_hbm,
    near_hbm,
    near_list_hbm,
    out_ref,
    charges,
    basis,
    transfer,
    far,
    coupling,
    near,
    counts,
    far_list,
    far_slot,
    rows,
    near_list,
    masked,
    halo,
    own,
    own_flat,
    stage,
    arrived,
    tail_in,
    up_own,
    up_in,
    cells,
    window,
    tail,
    up_all,
    coarse,
    near_sum,
    load_sem,
    halo_send,
    halo_recv,
    win_send,
    win_recv,
    tail_send,
    tail_recv,
    up_send,
    up_recv,
):
    box = lax.axis_index("box")
    lvl = lax.axis_index("lvl")
    me = box * lvl_count + lvl
    leaf_dev, points, rank = basis.shape
    columns = charges.shape[0]
    pairs = leaf_dev // 2
    edge = HALO // 2
    far_count = far.shape[1]
    win_count = far_list.shape[1]
    near_count = near.shape[1]
    near_even = near_count // 2 * 2
    cap = rows.shape[1]
    parents = coarse.shape[0]
    group = coupling.shape[1]
    wide = 2 * points
    cell_ring = cells.shape[0]
    win_ring = window.shape[0]
    cell_home = lax.rem(me, 2) * leaf_dev
    cell_away = leaf_dev - cell_home
    blocks = win_ring // leaf_dev
    win_home = lax.rem(me, blocks) * leaf_dev
    win_prev_home = lax.rem(me + blocks - 1, blocks) * leaf_dev
    win_next_home = lax.rem(me + 1, blocks) * leaf_dev

    loads = {}
    for i, (source, target) in enumerate(
        (
            (charges_hbm, charges),
            (counts_hbm, counts),
            (basis_hbm, basis),
            (rows_hbm, rows),
            (transfer_hbm, transfer),
            (near_list_hbm, near_list),
            (near_hbm, near),
            (coarse_hbm, coupling),
            (far_list_hbm, far_list),
            (far_slot_hbm, far_slot),
            (far_hbm, far),
        )
    ):
        loads[i] = pltpu.make_async_copy(source, target, load_sem.at[i])
        loads[i].start()

    def place(index):
        return {"box": lax.div(index, lvl_count), "lvl": lax.rem(index, lvl_count)}

    def other(step):
        return lax.rem(me + step, index_count)

    barrier = pltpu.get_barrier_semaphore()

    @pl.loop(1, index_count)
    def _(step):
        pl.semaphore_signal(barrier, inc=1, device_id=place(other(step)), device_id_type=MESH)

    has_prev = me > 0
    has_next = me < index_count - 1
    prev_place = place(lax.max(me - 1, 0))
    next_place = place(lax.min(me + 1, index_count - 1))

    def remote(source, target, send, recv, where):
        return pltpu.make_async_remote_copy(
            src_ref=source,
            dst_ref=target,
            send_sem=send,
            recv_sem=recv,
            device_id=where,
            device_id_type=MESH,
        )

    halo_next = remote(
        masked.at[pl.ds(pairs - edge, edge)], halo.at[0], halo_send.at[0], halo_recv.at[0], next_place
    )
    halo_prev = remote(masked.at[pl.ds(0, edge)], halo.at[1], halo_send.at[1], halo_recv.at[1], prev_place)
    win_next = remote(own, arrived.at[0], win_send.at[0], win_recv.at[0], next_place)
    win_prev = remote(own, arrived.at[1], win_send.at[1], win_recv.at[1], prev_place)

    def tail_copy(step):
        peer = other(step)
        return remote(
            stage.at[pl.ds(peer * cap, cap)],
            tail_in.at[pl.ds(me * cap, cap)],
            tail_send.at[step],
            tail_recv.at[step],
            place(peer),
        )

    def up_copy(step):
        return remote(
            up_own,
            up_in.at[lvl],
            up_send.at[step],
            up_recv.at[step],
            {"lvl": lax.rem(lvl + step, lvl_count)},
        )

    lanes = lax.broadcasted_iota(jnp.int32, (columns, wide), 1)

    def live(pair):
        first = counts[2 * pair]
        second = counts[2 * pair + 1] + points
        return (lanes < first) | ((lanes >= points) & (lanes < second))

    def spread(pair_block, target, at):
        turned = pair_block.T
        target[at] = turned[:points]
        target[at + 1] = turned[points:]

    loads[0].wait()
    loads[1].wait()

    for pair in range(pairs):
        block = charges[:, pair * wide : (pair + 1) * wide]
        masked[pair] = jnp.where(live(pair), block.astype(jnp.float32), 0.0).astype(jnp.bfloat16)

    loads[2].wait()

    for pair in range(pairs):
        block = masked[pair]
        first = nn(block[:, :points], basis[2 * pair])
        second = nn(block[:, points:], basis[2 * pair + 1])
        own[pair] = packed([first, second]).astype(jnp.bfloat16)
        for half, value in enumerate((first, second)):
            value = value.astype(jnp.bfloat16)
            own_flat[2 * pair + half] = packed([value[: columns // 2], value[columns // 2 :]])

    pl.semaphore_wait(barrier, index_count - 1)

    @pl.when(has_next)
    def _():
        halo_next.start()
        win_next.start()

    @pl.when(has_prev)
    def _():
        halo_prev.start()
        win_prev.start()

    loads[4].wait()
    sums = []
    for parent in range(parents):
        total = None
        for k in range(FAMILY // 2):
            pair = parent * (FAMILY // 2) + k
            block = own[pair]
            term = nn(block[:, :rank], transfer[2 * pair]) + nn(block[:, rank:], transfer[2 * pair + 1])
            total = term if total is None else total + term
        sums.append(total)
    for half in range(parents // 2):
        value = packed(sums[2 * half : 2 * half + 2]).astype(jnp.bfloat16)
        up_own[half] = value
        up_in[lvl, half] = value

    @pl.loop(1, lvl_count)
    def _(step):
        up_copy(step).start()

    loads[3].wait()

    @pl.loop(1, index_count)
    def _(step):
        peer = other(step)
        for j in range(cap):
            stage[peer * cap + j] = own_flat[rows[0, j, peer]]
        tail_copy(step).start()

    for j in range(cap):
        tail_in[me * cap + j] = own_flat[rows[0, j, me]]

    for pair in range(pairs):
        spread(masked[pair], cells, cell_home + 2 * pair)
        spread(own[pair], window, win_home + 2 * pair)

    loads[5].wait()
    loads[6].wait()

    @pl.when(has_prev)
    def _():
        halo_next.wait_recv()
        for pair in range(edge):
            spread(halo[0, pair], cells, cell_away + leaf_dev - HALO + 2 * pair)

    @pl.when(has_next)
    def _():
        halo_prev.wait_recv()
        for pair in range(edge):
            spread(halo[1, pair], cells, cell_away + 2 * pair)

    @pl.loop(0, pairs, unroll=8)
    def _(pair):
        for half in range(2):
            leaf = 2 * pair + half
            found = [cells[near_list[leaf, k] & (cell_ring - 1)] for k in range(near_count)]
            total = nn(packed([near[leaf, k] for k in range(near_even)]), stacked(found[:near_even]))
            for k in range(near_even, near_count):
                total = total + nn(near[leaf, k], found[k])
            near_sum[leaf] = total

    for i in (7, 8, 9, 10):
        loads[i].wait()

    @pl.loop(1, lvl_count)
    def _(step):
        up_copy(step).wait_recv()

    for peer in range(lvl_count):
        for half in range(parents // 2):
            spread(up_in[peer, half], up_all, peer * parents + 2 * half)

    for parent in range(parents):
        total = None
        for k in range(group):
            term = nn(coupling[parent, k], up_all[k])
            total = term if total is None else total + term
        coarse[parent] = total.astype(jnp.bfloat16)

    @pl.loop(1, index_count)
    def _(step):
        tail_copy(step).wait_recv()

    @pl.loop(0, index_count * cap, unroll=4)
    def _(slot):
        turned = tail_in[slot].T
        tail[slot] = packed([turned[:rank], turned[rank:]])

    @pl.when(has_prev)
    def _():
        win_next.wait_recv()
        for pair in range(pairs):
            spread(arrived[0, pair], window, win_prev_home + 2 * pair)

    @pl.when(has_next)
    def _():
        win_prev.wait_recv()
        for pair in range(pairs):
            spread(arrived[1, pair], window, win_next_home + 2 * pair)

    @pl.loop(0, pairs, unroll=8)
    def _(pair):
        parts = []
        for half in range(2):
            leaf = 2 * pair + half
            found = [window[far_list[leaf, k] & (win_ring - 1)] for k in range(win_count)]
            found += [tail[far_slot[k, leaf]] for k in range(far_count - win_count)]
            total = nn(transfer[leaf], coarse[lax.div(pair, FAMILY // 2)])
            total = total + nn(packed([far[leaf, k] for k in range(far_count)]), stacked(found))
            parts.append(near_sum[leaf] + nn(basis[leaf], total.astype(jnp.bfloat16)))
        total = jnp.where(live(pair), stacked(parts).T, 0.0)
        out_ref[:, pl.ds(pl.multiple_of(pair * wide, wide), wide)] = total.astype(jnp.bfloat16)

    @pl.when(has_next)
    def _():
        halo_next.wait_send()
        win_next.wait_send()

    @pl.when(has_prev)
    def _():
        halo_prev.wait_send()
        win_prev.wait_send()

    @pl.loop(1, index_count)
    def _(step):
        tail_copy(step).wait_send()

    @pl.loop(1, lvl_count)
    def _(step):
        up_copy(step).wait_send()


def on_device(
    lvl_count,
    index_count,
    charges,
    counts,
    basis,
    transfer,
    far_coupling,
    far_list,
    far_slot,
    send_rows,
    coarse_coupling,
    near_blocks,
    near_list,
):
    columns = charges.shape[0]
    leaf_dev, points, rank = basis.shape
    parents, group = coarse_coupling.shape[:2]
    cap = send_rows.shape[2]
    far_slot = far_slot.T
    send_rows = send_rows.transpose(0, 2, 1)
    half = jnp.bfloat16

    pairs = leaf_dev // 2

    def turned(count):
        return pltpu.VMEM((count, rank, columns), half)

    dma = pltpu.SemaphoreType.DMA
    return pl.pallas_call(
        functools.partial(kernel, lvl_count, index_count),
        out_shape=jax.ShapeDtypeStruct(charges.shape, half),
        in_specs=[pl.BlockSpec(memory_space=pl.ANY)] * 11,
        out_specs=pl.BlockSpec(memory_space=pltpu.VMEM),
        scratch_shapes=[
            pltpu.VMEM(charges.shape, half),
            pltpu.VMEM(basis.shape, half),
            pltpu.VMEM(transfer.shape, half),
            pltpu.VMEM(far_coupling.shape, half),
            pltpu.VMEM(coarse_coupling.shape, half),
            pltpu.VMEM(near_blocks.shape, half),
            pltpu.SMEM(counts.shape, jnp.int32),
            pltpu.SMEM(far_list.shape, jnp.int32),
            pltpu.SMEM(far_slot.shape, jnp.int32),
            pltpu.SMEM(send_rows.shape, jnp.int32),
            pltpu.SMEM(near_list.shape, jnp.int32),
            pltpu.VMEM((pairs, columns, 2 * points), half),
            pltpu.VMEM((2, HALO // 2, columns, 2 * points), half),
            pltpu.VMEM((pairs, columns, 2 * rank), half),
            pltpu.VMEM((leaf_dev, columns // 2, 2 * rank), half),
            pltpu.VMEM((index_count * cap, columns // 2, 2 * rank), half),
            pltpu.VMEM((2, pairs, columns, 2 * rank), half),
            pltpu.VMEM((index_count * cap, columns // 2, 2 * rank), half),
            pltpu.VMEM((parents // 2, columns, 2 * rank), half),
            pltpu.VMEM((lvl_count, parents // 2, columns, 2 * rank), half),
            turned(2 * leaf_dev),
            turned(4 * leaf_dev),
            turned(index_count * cap),
            turned(group),
            turned(parents),
            pltpu.VMEM((leaf_dev, points, columns), jnp.float32),
            dma((11,)),
            dma((2,)),
            dma((2,)),
            dma((2,)),
            dma((2,)),
            dma((index_count,)),
            dma((index_count,)),
            dma((lvl_count,)),
            dma((lvl_count,)),
        ],
        compiler_params=pltpu.CompilerParams(
            collective_id=0, has_side_effects=True, vmem_limit_bytes=63 * 1024 * 1024
        ),
    )(
        charges,
        counts,
        basis,
        transfer,
        far_coupling,
        far_list,
        far_slot,
        send_rows,
        coarse_coupling,
        near_blocks,
        near_list,
    )


def solution(mesh):
    every = ("grp", "box", "lvl")
    placed = (
        P("rhs", every),
        P(every),
        P(every, None, None),
        P(every, None, None),
        P(every, None, None, None),
        P(every, None),
        P(every, None),
        P(every, None, None),
        P(every, None, None, None),
        P(every, None, None, None),
        P(every, None),
    )
    lvl_count = mesh.shape["lvl"]
    return jax.shard_map(
        functools.partial(on_device, lvl_count, lvl_count * mesh.shape["box"]),
        mesh=mesh,
        in_specs=placed,
        out_specs=P("rhs", every),
        check_vma=False,
    )
```

```python
import functools

import jax
import jax.numpy as jnp
from jax import lax
from jax.experimental import pallas as pl
from jax.experimental.pallas import tpu as pltpu
from jax.sharding import PartitionSpec as P

HALO = 4
FAMILY = 8
MESH = pl.DeviceIdType.MESH


def nn(a, b):
    return lax.dot_general(a, b, (((1,), (0,)), ((), ())), preferred_element_type=jnp.float32)


def packed(blocks):
    return jnp.concatenate(blocks, axis=1)


def stacked(blocks):
    return jnp.concatenate(blocks, axis=0)


def kernel(
    lvl_count,
    index_count,
    charges_hbm,
    counts_hbm,
    basis_hbm,
    transfer_hbm,
    far_hbm,
    far_list_hbm,
    far_slot_hbm,
    rows_hbm,
    coarse_hbm,
    near_hbm,
    near_list_hbm,
    out_ref,
    charges,
    basis,
    transfer,
    far,
    coupling,
    near,
    counts,
    far_list,
    far_slot,
    rows,
    near_list,
    masked,
    halo,
    own,
    own_flat,
    stage,
    arrived,
    tail_in,
    up_own,
    up_in,
    cells,
    window,
    tail,
    up_all,
    coarse,
    near_sum,
    load_sem,
    halo_send,
    halo_recv,
    win_send,
    win_recv,
    tail_send,
    tail_recv,
    up_send,
    up_recv,
):
    box = lax.axis_index("box")
    lvl = lax.axis_index("lvl")
    me = box * lvl_count + lvl
    leaf_dev, points, rank = basis.shape
    columns = charges.shape[0]
    pairs = leaf_dev // 2
    edge = HALO // 2
    far_count = far.shape[1]
    win_count = far_list.shape[1]
    near_count = near.shape[1]
    near_even = near_count // 2 * 2
    cap = rows.shape[1]
    parents = coarse.shape[0]
    group = coupling.shape[1]
    wide = 2 * points
    cell_ring = cells.shape[0]
    win_ring = window.shape[0]
    cell_home = lax.rem(me, 2) * leaf_dev
    cell_away = leaf_dev - cell_home
    blocks = win_ring // leaf_dev
    win_home = lax.rem(me, blocks) * leaf_dev
    win_prev_home = lax.rem(me + blocks - 1, blocks) * leaf_dev
    win_next_home = lax.rem(me + 1, blocks) * leaf_dev

    loads = {}
    for i, (source, target) in enumerate(
        (
            (charges_hbm, charges),
            (counts_hbm, counts),
            (basis_hbm, basis),
            (rows_hbm, rows),
            (transfer_hbm, transfer),
            (near_list_hbm, near_list),
            (near_hbm, near),
            (coarse_hbm, coupling),
            (far_list_hbm, far_list),
            (far_slot_hbm, far_slot),
            (far_hbm, far),
        )
    ):
        loads[i] = pltpu.make_async_copy(source, target, load_sem.at[i])
        loads[i].start()

    def place(index):
        return {"box": lax.div(index, lvl_count), "lvl": lax.rem(index, lvl_count)}

    def other(step):
        return lax.rem(me + step, index_count)

    barrier = pltpu.get_barrier_semaphore()

    @pl.loop(1, index_count)
    def _(step):
        pl.semaphore_signal(barrier, inc=1, device_id=place(other(step)), device_id_type=MESH)

    has_prev = me > 0
    has_next = me < index_count - 1
    prev_place = place(lax.max(me - 1, 0))
    next_place = place(lax.min(me + 1, index_count - 1))

    def remote(source, target, send, recv, where):
        return pltpu.make_async_remote_copy(
            src_ref=source,
            dst_ref=target,
            send_sem=send,
            recv_sem=recv,
            device_id=where,
            device_id_type=MESH,
        )

    halo_next = remote(
        masked.at[pl.ds(pairs - edge, edge)], halo.at[0], halo_send.at[0], halo_recv.at[0], next_place
    )
    halo_prev = remote(masked.at[pl.ds(0, edge)], halo.at[1], halo_send.at[1], halo_recv.at[1], prev_place)
    win_next = remote(own, arrived.at[0], win_send.at[0], win_recv.at[0], next_place)
    win_prev = remote(own, arrived.at[1], win_send.at[1], win_recv.at[1], prev_place)

    def tail_copy(step):
        peer = other(step)
        return remote(
            stage.at[pl.ds(peer * cap, cap)],
            tail_in.at[pl.ds(me * cap, cap)],
            tail_send.at[step],
            tail_recv.at[step],
            place(peer),
        )

    def up_copy(step):
        return remote(
            up_own,
            up_in.at[lvl],
            up_send.at[step],
            up_recv.at[step],
            {"lvl": lax.rem(lvl + step, lvl_count)},
        )

    lanes = lax.broadcasted_iota(jnp.int32, (columns, wide), 1)

    def live(pair):
        first = counts[2 * pair]
        second = counts[2 * pair + 1] + points
        return (lanes < first) | ((lanes >= points) & (lanes < second))

    def spread(pair_block, target, at):
        turned = pair_block.T
        target[at] = turned[:points]
        target[at + 1] = turned[points:]

    loads[0].wait()
    loads[1].wait()

    for pair in range(pairs):
        block = charges[:, pair * wide : (pair + 1) * wide]
        masked[pair] = jnp.where(live(pair), block.astype(jnp.float32), 0.0).astype(jnp.bfloat16)

    loads[2].wait()

    for pair in range(pairs):
        block = masked[pair]
        first = nn(block[:, :points], basis[2 * pair])
        second = nn(block[:, points:], basis[2 * pair + 1])
        own[pair] = packed([first, second]).astype(jnp.bfloat16)
        for half, value in enumerate((first, second)):
            value = value.astype(jnp.bfloat16)
            own_flat[2 * pair + half] = packed([value[: columns // 2], value[columns // 2 :]])

    pl.semaphore_wait(barrier, index_count - 1)

    @pl.when(has_next)
    def _():
        halo_next.start()
        win_next.start()

    @pl.when(has_prev)
    def _():
        halo_prev.start()
        win_prev.start()

    loads[4].wait()
    sums = []
    for parent in range(parents):
        total = None
        for k in range(FAMILY // 2):
            pair = parent * (FAMILY // 2) + k
            block = own[pair]
            term = nn(block[:, :rank], transfer[2 * pair]) + nn(block[:, rank:], transfer[2 * pair + 1])
            total = term if total is None else total + term
        sums.append(total)
    for half in range(parents // 2):
        value = packed(sums[2 * half : 2 * half + 2]).astype(jnp.bfloat16)
        up_own[half] = value
        up_in[lvl, half] = value

    @pl.loop(1, lvl_count)
    def _(step):
        up_copy(step).start()

    loads[3].wait()

    @pl.loop(1, index_count)
    def _(step):
        peer = other(step)
        for j in range(cap):
            stage[peer * cap + j] = own_flat[rows[0, j, peer]]
        tail_copy(step).start()

    for j in range(cap):
        tail_in[me * cap + j] = own_flat[rows[0, j, me]]

    for pair in range(pairs):
        spread(masked[pair], cells, cell_home + 2 * pair)
        spread(own[pair], window, win_home + 2 * pair)

    loads[5].wait()
    loads[6].wait()

    def near_pair(pair):
        for half in range(2):
            leaf = 2 * pair + half
            found = [cells[near_list[leaf, k] & (cell_ring - 1)] for k in range(near_count)]
            total = nn(packed([near[leaf, k] for k in range(near_even)]), stacked(found[:near_even]))
            for k in range(near_even, near_count):
                total = total + nn(near[leaf, k], found[k])
            near_sum[leaf] = total

    for pair in range(edge, pairs - edge):
        near_pair(pair)

    @pl.when(has_prev)
    def _():
        halo_next.wait_recv()
        for pair in range(edge):
            spread(halo[0, pair], cells, cell_away + leaf_dev - HALO + 2 * pair)

    @pl.when(has_next)
    def _():
        halo_prev.wait_recv()
        for pair in range(edge):
            spread(halo[1, pair], cells, cell_away + 2 * pair)

    for pair in (*range(edge), *range(pairs - edge, pairs)):
        near_pair(pair)

    for i in (7, 8, 9, 10):
        loads[i].wait()

    @pl.loop(1, lvl_count)
    def _(step):
        up_copy(step).wait_recv()

    for peer in range(lvl_count):
        for half in range(parents // 2):
            spread(up_in[peer, half], up_all, peer * parents + 2 * half)

    for parent in range(parents):
        total = None
        for k in range(group):
            term = nn(coupling[parent, k], up_all[k])
            total = term if total is None else total + term
        coarse[parent] = total.astype(jnp.bfloat16)

    @pl.loop(1, index_count)
    def _(step):
        tail_copy(step).wait_recv()

    @pl.loop(0, index_count * cap, unroll=4)
    def _(slot):
        turned = tail_in[slot].T
        tail[slot] = packed([turned[:rank], turned[rank:]])

    @pl.when(has_prev)
    def _():
        win_next.wait_recv()
        for pair in range(pairs):
            spread(arrived[0, pair], window, win_prev_home + 2 * pair)

    @pl.when(has_next)
    def _():
        win_prev.wait_recv()
        for pair in range(pairs):
            spread(arrived[1, pair], window, win_next_home + 2 * pair)

    @pl.loop(0, pairs, unroll=8)
    def _(pair):
        parts = []
        for half in range(2):
            leaf = 2 * pair + half
            found = [window[far_list[leaf, k] & (win_ring - 1)] for k in range(win_count)]
            found += [tail[far_slot[k, leaf]] for k in range(far_count - win_count)]
            total = nn(transfer[leaf], coarse[lax.div(pair, FAMILY // 2)])
            total = total + nn(packed([far[leaf, k] for k in range(far_count)]), stacked(found))
            parts.append(near_sum[leaf] + nn(basis[leaf], total.astype(jnp.bfloat16)))
        total = jnp.where(live(pair), stacked(parts).T, 0.0)
        out_ref[:, pl.ds(pl.multiple_of(pair * wide, wide), wide)] = total.astype(jnp.bfloat16)

    @pl.when(has_next)
    def _():
        halo_next.wait_send()
        win_next.wait_send()

    @pl.when(has_prev)
    def _():
        halo_prev.wait_send()
        win_prev.wait_send()

    @pl.loop(1, index_count)
    def _(step):
        tail_copy(step).wait_send()

    @pl.loop(1, lvl_count)
    def _(step):
        up_copy(step).wait_send()


def on_device(
    lvl_count,
    index_count,
    charges,
    counts,
    basis,
    transfer,
    far_coupling,
    far_list,
    far_slot,
    send_rows,
    coarse_coupling,
    near_blocks,
    near_list,
):
    columns = charges.shape[0]
    leaf_dev, points, rank = basis.shape
    parents, group = coarse_coupling.shape[:2]
    cap = send_rows.shape[2]
    far_slot = far_slot.T
    send_rows = send_rows.transpose(0, 2, 1)
    half = jnp.bfloat16

    pairs = leaf_dev // 2

    def turned(count):
        return pltpu.VMEM((count, rank, columns), half)

    dma = pltpu.SemaphoreType.DMA
    return pl.pallas_call(
        functools.partial(kernel, lvl_count, index_count),
        out_shape=jax.ShapeDtypeStruct(charges.shape, half),
        in_specs=[pl.BlockSpec(memory_space=pl.ANY)] * 11,
        out_specs=pl.BlockSpec(memory_space=pltpu.VMEM),
        scratch_shapes=[
            pltpu.VMEM(charges.shape, half),
            pltpu.VMEM(basis.shape, half),
            pltpu.VMEM(transfer.shape, half),
            pltpu.VMEM(far_coupling.shape, half),
            pltpu.VMEM(coarse_coupling.shape, half),
            pltpu.VMEM(near_blocks.shape, half),
            pltpu.SMEM(counts.shape, jnp.int32),
            pltpu.SMEM(far_list.shape, jnp.int32),
            pltpu.SMEM(far_slot.shape, jnp.int32),
            pltpu.SMEM(send_rows.shape, jnp.int32),
            pltpu.SMEM(near_list.shape, jnp.int32),
            pltpu.VMEM((pairs, columns, 2 * points), half),
            pltpu.VMEM((2, HALO // 2, columns, 2 * points), half),
            pltpu.VMEM((pairs, columns, 2 * rank), half),
            pltpu.VMEM((leaf_dev, columns // 2, 2 * rank), half),
            pltpu.VMEM((index_count * cap, columns // 2, 2 * rank), half),
            pltpu.VMEM((2, pairs, columns, 2 * rank), half),
            pltpu.VMEM((index_count * cap, columns // 2, 2 * rank), half),
            pltpu.VMEM((parents // 2, columns, 2 * rank), half),
            pltpu.VMEM((lvl_count, parents // 2, columns, 2 * rank), half),
            turned(2 * leaf_dev),
            turned(4 * leaf_dev),
            turned(index_count * cap),
            turned(group),
            turned(parents),
            pltpu.VMEM((leaf_dev, points, columns), jnp.float32),
            dma((11,)),
            dma((2,)),
            dma((2,)),
            dma((2,)),
            dma((2,)),
            dma((index_count,)),
            dma((index_count,)),
            dma((lvl_count,)),
            dma((lvl_count,)),
        ],
        compiler_params=pltpu.CompilerParams(
            collective_id=0, has_side_effects=True, vmem_limit_bytes=63 * 1024 * 1024
        ),
    )(
        charges,
        counts,
        basis,
        transfer,
        far_coupling,
        far_list,
        far_slot,
        send_rows,
        coarse_coupling,
        near_blocks,
        near_list,
    )


def solution(mesh):
    every = ("grp", "box", "lvl")
    placed = (
        P("rhs", every),
        P(every),
        P(every, None, None),
        P(every, None, None),
        P(every, None, None, None),
        P(every, None),
        P(every, None),
        P(every, None, None),
        P(every, None, None, None),
        P(every, None, None, None),
        P(every, None),
    )
    lvl_count = mesh.shape["lvl"]
    return jax.shard_map(
        functools.partial(on_device, lvl_count, lvl_count * mesh.shape["box"]),
        mesh=mesh,
        in_specs=placed,
        out_specs=P("rhs", every),
        check_vma=False,
    )
```
